32 devices in a mesh: row: 4 (over y, x), col: 8 (over z, core).
Axes of the slice: x: 2, y: 2, z: 4, core: 2. Of those that a mesh axis runs over, the one named last changes fastest.
Arguments:
- gram: float32 [4096, 4096], P('row', 'col'), may hold values from -6 to 8
- rotations: float32 [2, 4, 1024, 1024], P(None, 'row', 'col'), may hold values from -1 to 2
Outputs:
- rotated: float32 [4096, 4096], P('row', 'col')
The draws below stay inside these ranges and needn't reach their ends.
All inputs are finite; a program needn't handle non-finite values.
Results may differ from the reference program's by a relative error of at most 0.00016.
Values sent between devices are 32-bit elements; how exact they have to be, the bound alone decides.
A program may use at most 64 MiB of HBM per device.

```python
import jax
import jax.numpy as jnp
import numpy as np
from jax import lax

BLOCK = 512
STEPS = 2
PAIRS = 4
ORDER = 4096


def draw_gram(key, part):
    first = jax.random.fold_in(key, 0)
    base = jnp.clip(jax.random.normal(first, (ORDER, ORDER), jnp.float32), -5.0, 5.0)
    sym = 0.5 * (base + base.T)
    return sym + 2.0 * jnp.eye(ORDER, dtype=jnp.float32)


def draw_rotations(key, part):
    size = 2 * BLOCK
    sigma = 0.5 / size ** 0.5
    shape = (STEPS, PAIRS, size, size)
    noise = jnp.clip(jax.random.normal(key, shape, jnp.float32), -6.0, 6.0) * sigma
    return noise + jnp.eye(size, dtype=jnp.float32)


def setup_inputs(seed: int = 0) -> dict:
    splits = jax.random.split(jax.random.key(seed), 3)
    return {
        "gram": draw_gram(jax.random.fold_in(splits[2], 71), 0),
        "rotations": draw_rotations(jax.random.fold_in(splits[2], 71), 0),
    }


def move_order(pair_count):
    order = np.zeros(2 * pair_count, dtype=np.int32)
    for pair in range(pair_count):
        if pair == 0:
            order[0] = 0
        elif pair == 1:
            order[2] = 1
        else:
            order[2 * pair] = 2 * pair - 2
        if pair < pair_count - 1:
            order[2 * pair + 1] = 2 * pair + 3
        else:
            order[2 * pair + 1] = 2 * pair
    return order


def reference(gram, rotations):
    pair_count = PAIRS
    blocks = 2 * pair_count
    order = jnp.asarray(move_order(pair_count))
    current = gram
    for step in range(STEPS):
        turn = rotations[step].astype(jnp.float32)
        cols = current.reshape(ORDER, pair_count, 2 * BLOCK)
        cols = jnp.einsum("npa,pab->npb", cols, turn, precision=lax.Precision.HIGHEST)
        current = cols.reshape(ORDER, ORDER)
        rows = current.reshape(pair_count, 2 * BLOCK, ORDER)
        rows = jnp.einsum("pab,pan->pbn", turn, rows, precision=lax.Precision.HIGHEST)
        tiles = rows.reshape(blocks, BLOCK, blocks, BLOCK)
        tiles = jnp.take(tiles, order, axis=0)
        tiles = jnp.take(tiles, order, axis=2)
        current = tiles.reshape(ORDER, ORDER)
    return current
```

```python
import functools

import jax
import jax.numpy as jnp
from jax import lax
from jax.experimental import pallas as pl
from jax.experimental.pallas import tpu as pltpu
from jax.sharding import PartitionSpec as P

MESH = pl.DeviceIdType.MESH
TILE = 256


def pick(cond, yes, no):
    return jnp.where(cond, jnp.int32(yes), jnp.int32(no))


def goes_to(n, pair, odd):
    even_pair = pick(pair == 0, 0, pick(pair == n - 1, n - 1, pair + 1))
    even_half = pick(pair == n - 1, 1, 0)
    odd_pair = pick(pair == 0, 1, pair - 1)
    odd_half = pick(pair == 0, 0, 1)
    return pick(odd == 0, even_pair, odd_pair), pick(odd == 0, even_half, odd_half)


def comes_from(n, pair, odd):
    even_pair = pick(pair == 0, 0, pair - 1)
    even_half = pick(pair == 1, 1, 0)
    odd_pair = pick(pair == n - 1, n - 1, pair + 1)
    odd_half = pick(pair == n - 1, 0, 1)
    return pick(odd == 0, even_pair, odd_pair), pick(odd == 0, even_half, odd_half)


def ring_next(n, r, direction):
    order = [i ^ (i >> 1) for i in range(n)]
    result = jnp.int32(0)
    for i in range(n):
        result = pick(r == order[i], order[(i + direction) % n], result)
    return result


def split(x):
    hi = x.astype(jnp.bfloat16)
    lo = (x - hi.astype(jnp.float32)).astype(jnp.bfloat16)
    return hi, lo


def dot(a, b):
    return jnp.dot(a, b, preferred_element_type=jnp.float32)


def kernel(
    n, gram, rot, out, X, V, T, C, res, Xh, Xl, Bh, Bl,
    xsend, xrecv, vsend, vrecv, tsend, trecv, msend, mrecv,
):
    r = lax.axis_index("row")
    c = lax.axis_index("col")
    z = c // 2
    p = c % 2
    steps, h, size = rot.shape
    half = size // 2
    succ = ring_next(n, r, 1)
    pred = ring_next(n, r, -1)
    partner = (r, c + 1 - 2 * p)
    up = (r, c + 2)
    down = (r, c - 2)
    is_root = r == z
    pending = []

    def remote(src, dst, send, recv, device):
        return pltpu.make_async_remote_copy(
            src_ref=src, dst_ref=dst, send_sem=send, recv_sem=recv,
            device_id=device, device_id_type=MESH,
        )

    def x_rows(s, cc):
        return X.at[s, pl.ds(pl.multiple_of(cc * h, h), h), :]

    def x_copy(s, cc, way):
        device = (up, down, partner)[way]
        rows = x_rows(s, cc)
        return remote(rows, rows, xsend.at[s, cc, way], xrecv.at[s, cc], device)

    def v_copy(s, cc, q, root):
        rows = pl.ds(pl.multiple_of(cc * h, h), h)
        dst = V.at[s, rows, :]
        src = X.at[s, rows, pl.ds(pl.multiple_of(p * half, half), half)] if root else dst
        device = ((succ if q == 0 else pred), c)
        return remote(src, dst, vsend.at[s, cc], vrecv.at[s, cc], device)

    def go(cond, make):
        def begin():
            make().start()
        def end():
            make().wait_send()
        if cond is None:
            begin()
        else:
            pl.when(cond)(begin)
        pending.append((cond, end))

    targets = []
    to_pair, to_odd = goes_to(n, z, p)
    to_col = 2 * to_pair + to_odd
    for a in range(2):
        to_row, slot = goes_to(n, r, jnp.int32(a))
        stays = jnp.logical_and(to_row == r, to_col == c)
        targets.append((to_row, slot, stays))
    origins = []
    from_pair, from_odd = comes_from(n, z, p)
    from_col = 2 * from_pair + from_odd
    for a in range(2):
        from_row, _ = comes_from(n, r, jnp.int32(a))
        stays = jnp.logical_and(from_row == r, from_col == c)
        origins.append((from_row, stays))

    barrier = pltpu.get_barrier_semaphore()

    def hello(device):
        pl.semaphore_signal(barrier, inc=1, device_id=device, device_id_type=MESH)

    count = jnp.int32(3)
    hello(partner)
    hello((succ, c))
    hello((pred, c))
    pl.when(z < n - 1)(lambda: hello(up))
    pl.when(z > 0)(lambda: hello(down))
    count = count + pick(z < n - 1, 1, 0) + pick(z > 0, 1, 0)
    for a in range(2):
        to_row, _, stays = targets[a]
        pl.when(jnp.logical_not(stays))(lambda to_row=to_row: hello((to_row, to_col)))
        count = count + pick(stays, 0, 1)
        from_row, stays = origins[a]
        pl.when(jnp.logical_not(stays))(lambda from_row=from_row: hello((from_row, from_col)))
        count = count + pick(stays, 0, 1)
    pl.semaphore_wait(barrier, count)

    def roots(s, zs, cond):
        for q in range(2):
            here = is_root if cond is None else jnp.logical_and(is_root, cond)
            go(here, lambda q=q: v_copy(s, 2 * zs + q, q, True))

    def start_own(s):
        X[s, pl.ds(pl.multiple_of(c * h, h), h), :] = rot[s]
        go(z < n - 1, lambda: x_copy(s, c, 0))
        go(z > 0, lambda: x_copy(s, c, 1))
        go(None, lambda: x_copy(s, c, 2))

    def finish_own(s):
        x_copy(s, 2 * z + 1 - p, 2).wait_recv()
        roots(s, z, None)

    def sides(d):
        return ((0, z - d, z >= d), (1, z + d, z + d < n))

    def service(s, d):
        for way, zs, exists in sides(d):
            cc = 2 * zs + p
            pl.when(exists)(lambda cc=cc, way=way: x_copy(s, cc, way).wait_recv())
            if d < n - 1:
                onward = z < n - 1 if way == 0 else z > 0
                go(jnp.logical_and(exists, onward), lambda cc=cc, way=way: x_copy(s, cc, way))
            go(exists, lambda cc=cc: x_copy(s, cc, 2))
        for way, zs, exists in sides(d):
            cc = 2 * zs + 1 - p
            pl.when(exists)(lambda cc=cc: x_copy(s, cc, 2).wait_recv())
            roots(s, zs, exists)

    def relay(s, d):
        group = ((0, z, None),) if d == 0 else sides(d)
        for _, zs, exists in group:
            for q in range(2):
                cc = 2 * zs + q
                here = jnp.logical_not(is_root)
                if exists is not None:
                    here = jnp.logical_and(here, exists)
                pl.when(here)(lambda cc=cc, q=q: v_copy(s, cc, q, False).wait_recv())
                further = (succ if q == 0 else pred) != z
                go(jnp.logical_and(here, further), lambda cc=cc, q=q: v_copy(s, cc, q, False))

    def split_x(s):
        @pl.loop(0, size // TILE)
        def _(i):
            rows = pl.ds(pl.multiple_of(i * TILE, TILE), TILE)
            hi, lo = split(X[s, rows, :].T)
            Xh[:, rows] = hi
            Xl[:, rows] = lo

    def split_b(load):
        @pl.loop(0, size // TILE)
        def _(i):
            rows = pl.ds(pl.multiple_of(i * TILE, TILE), TILE)
            hi, lo = split(load(rows))
            Bh[rows, :] = hi
            Bl[rows, :] = lo

    def split_v(s):
        columns = pl.ds(pl.multiple_of(p * half, half), half)
        pl.when(is_root)(lambda: split_b(lambda rows: X[s, rows, columns]))
        pl.when(jnp.logical_not(is_root))(lambda: split_b(lambda rows: V[s, rows, :]))

    def t_copy(s, a):
        part = T.at[s, p, pl.ds(a * half, half), :]
        return remote(part, part, tsend.at[s, a], trecv.at[s, a], partner)

    def turn(s):
        for a in range(2):
            @pl.loop(0, half // TILE)
            def _(i):
                rows = pl.ds(pl.multiple_of(a * half + i * TILE, TILE), TILE)
                hi = Xh[rows, :]
                T[s, p, rows, :] = dot(hi, Bh[...]) + dot(hi, Bl[...]) + dot(Xl[rows, :], Bh[...])
            go(None, lambda a=a: t_copy(s, a))

    def m_copy(s, a):
        to_row, slot, _ = targets[a]
        landing = C if s < steps - 1 else out
        dst = landing.at[pl.ds(pl.multiple_of(slot * half, half), half), :] if s == steps - 1 \
            else landing.at[s, pl.ds(pl.multiple_of(slot * half, half), half), :]
        src = res.at[s, pl.ds(a * half, half), :]
        return src, dst, slot, to_row

    def m_remote(s, a):
        src, dst, slot, to_row = m_copy(s, a)
        return remote(src, dst, msend.at[s, a], mrecv.at[s, slot], (to_row, to_col))

    def m_local(s, a):
        src, dst, slot, _ = m_copy(s, a)
        return pltpu.make_async_copy(src, dst, mrecv.at[s, slot])

    def mix(s):
        for a in range(2):
            t_copy(s, a).wait_recv()

            @pl.loop(0, half // TILE)
            def _(i):
                rows = pl.ds(pl.multiple_of(a * half + i * TILE, TILE), TILE)
                total = jnp.zeros((TILE, half), jnp.float32)
                for q in range(2):
                    hi, lo = split(T[s, q, rows, :])
                    bh = Bh[q * half:(q + 1) * half, :]
                    bl = Bl[q * half:(q + 1) * half, :]
                    total = total + (dot(hi, bh) + dot(hi, bl) + dot(lo, bh))
                res[s, rows, :] = total
            stays = targets[a][2]
            pl.when(stays)(lambda a=a: m_local(s, a).start())
            go(jnp.logical_not(stays), lambda a=a: m_remote(s, a))

    def arrive(s):
        for a in range(2):
            src = res.at[s, pl.ds(0, half), :]
            dst = (C.at[s] if s < steps - 1 else out).at[pl.ds(a * half, half), :]
            pltpu.make_async_copy(src, dst, mrecv.at[s, a]).wait()

    start_own(0)
    finish_own(0)
    for d in range(1, n):
        service(0, d)
        if d == n - 2 or n == 2:
            start_own(1)
        if d >= 2:
            relay(0, d - 2)
    split_x(0)
    split_b(lambda rows: gram[rows, :])
    turn(0)
    for d in range(max(n - 2, 0), n - 1):
        relay(0, d)
    finish_own(1)
    service(1, 1)
    relay(0, n - 1)
    split_v(0)
    mix(0)
    for d in range(2, n):
        service(1, d)
        relay(1, d - 2)
    split_x(1)
    for d in range(max(n - 2, 0), n):
        relay(1, d)
    arrive(0)
    split_b(lambda rows: C[0, rows, :])
    turn(1)
    split_v(1)
    mix(1)
    arrive(1)
    for cond, end in pending:
        if cond is None:
            end()
        else:
            pl.when(cond)(end)


def shards(gram, rotations):
    n = lax.axis_size("row")
    n_col = lax.axis_size("col")
    steps, _, h, size = rotations.shape
    half = size // 2
    f32, bf16 = jnp.float32, jnp.bfloat16
    dma = pltpu.SemaphoreType.DMA
    vmem = pl.BlockSpec(memory_space=pltpu.VMEM)
    flops = steps * 2 * 2 * size * size * half * 3
    return pl.pallas_call(
        functools.partial(kernel, n),
        out_shape=jax.ShapeDtypeStruct(gram.shape, f32),
        in_specs=[vmem, vmem],
        out_specs=vmem,
        scratch_shapes=[
            pltpu.VMEM((steps, size, size), f32),
            pltpu.VMEM((steps, size, half), f32),
            pltpu.VMEM((steps, 2, size, half), f32),
            pltpu.VMEM((steps - 1, size, half), f32),
            pltpu.VMEM((steps, size, half), f32),
            pltpu.VMEM((size, size), bf16),
            pltpu.VMEM((size, size), bf16),
            pltpu.VMEM((size, half), bf16),
            pltpu.VMEM((size, half), bf16),
            dma((steps, n_col, 3)),
            dma((steps, n_col)),
            dma((steps, n_col)),
            dma((steps, n_col)),
            dma((steps, 2)),
            dma((steps, 2)),
            dma((steps, 2)),
            dma((steps, 2)),
        ],
        compiler_params=pltpu.CompilerParams(
            collective_id=0, has_side_effects=True, vmem_limit_bytes=56 * 1024 * 1024
        ),
        cost_estimate=pl.CostEstimate(flops=flops, bytes_accessed=8 * 1024 * 1024, transcendentals=0),
    )(gram, rotations.reshape(steps, h, size))


def solution(mesh):
    placed = (P("row", "col"), P(None, "row", "col", None))
    return jax.shard_map(
        shards, mesh=mesh, in_specs=placed, out_specs=P("row", "col"), check_vma=False
    )
```

```python
import functools

import jax
import jax.numpy as jnp
from jax import lax
from jax.experimental import pallas as pl
from jax.experimental.pallas import tpu as pltpu
from jax.sharding import PartitionSpec as P

MESH = pl.DeviceIdType.MESH
TILE = 256


def pick(cond, yes, no):
    return jnp.where(cond, jnp.int32(yes), jnp.int32(no))


def goes_to(n, pair, odd):
    even_pair = pick(pair == 0, 0, pick(pair == n - 1, n - 1, pair + 1))
    even_half = pick(pair == n - 1, 1, 0)
    odd_pair = pick(pair == 0, 1, pair - 1)
    odd_half = pick(pair == 0, 0, 1)
    return pick(odd == 0, even_pair, odd_pair), pick(odd == 0, even_half, odd_half)


def comes_from(n, pair, odd):
    even_pair = pick(pair == 0, 0, pair - 1)
    even_half = pick(pair == 1, 1, 0)
    odd_pair = pick(pair == n - 1, n - 1, pair + 1)
    odd_half = pick(pair == n - 1, 0, 1)
    return pick(odd == 0, even_pair, odd_pair), pick(odd == 0, even_half, odd_half)


def ring_next(n, r, direction):
    order = [i ^ (i >> 1) for i in range(n)]
    result = jnp.int32(0)
    for i in range(n):
        result = pick(r == order[i], order[(i + direction) % n], result)
    return result


def split(x):
    hi = x.astype(jnp.bfloat16)
    lo = (x - hi.astype(jnp.float32)).astype(jnp.bfloat16)
    return hi, lo


def dot(a, b):
    return jnp.dot(a, b, preferred_element_type=jnp.float32)


def kernel(
    n, gram, rot, out, X, V, T, C, res, Xh, Xl, Bh, Bl,
    xsend, xrecv, vsend, vrecv, tsend, trecv, msend, mrecv,
):
    r = lax.axis_index("row")
    c = lax.axis_index("col")
    z = c // 2
    p = c % 2
    steps, h, size = rot.shape
    half = size // 2
    succ = ring_next(n, r, 1)
    pred = ring_next(n, r, -1)
    partner = (r, c + 1 - 2 * p)
    up = (r, c + 2)
    down = (r, c - 2)
    is_root = r == z
    pending = []

    def remote(src, dst, send, recv, device):
        return pltpu.make_async_remote_copy(
            src_ref=src, dst_ref=dst, send_sem=send, recv_sem=recv,
            device_id=device, device_id_type=MESH,
        )

    def x_rows(s, cc):
        return X.at[s, pl.ds(pl.multiple_of(cc * h, h), h), :]

    def x_copy(s, cc, way):
        device = (up, down, partner)[way]
        rows = x_rows(s, cc)
        return remote(rows, rows, xsend.at[s, cc, way], xrecv.at[s, cc], device)

    def v_copy(s, cc, q, root):
        rows = pl.ds(pl.multiple_of(cc * h, h), h)
        dst = V.at[s, rows, :]
        src = X.at[s, rows, pl.ds(pl.multiple_of(p * half, half), half)] if root else dst
        device = ((succ if q == 0 else pred), c)
        return remote(src, dst, vsend.at[s, cc], vrecv.at[s, cc], device)

    def go(cond, make):
        def begin():
            make().start()
        def end():
            make().wait_send()
        if cond is None:
            begin()
        else:
            pl.when(cond)(begin)
        pending.append((cond, end))

    targets = []
    to_pair, to_odd = goes_to(n, z, p)
    to_col = 2 * to_pair + to_odd
    for a in range(2):
        to_row, slot = goes_to(n, r, jnp.int32(a))
        stays = jnp.logical_and(to_row == r, to_col == c)
        targets.append((to_row, slot, stays))
    origins = []
    from_pair, from_odd = comes_from(n, z, p)
    from_col = 2 * from_pair + from_odd
    for a in range(2):
        from_row, _ = comes_from(n, r, jnp.int32(a))
        stays = jnp.logical_and(from_row == r, from_col == c)
        origins.append((from_row, stays))

    barrier = pltpu.get_barrier_semaphore()

    def hello(device):
        pl.semaphore_signal(barrier, inc=1, device_id=device, device_id_type=MESH)

    count = jnp.int32(3)
    hello(partner)
    hello((succ, c))
    hello((pred, c))
    pl.when(z < n - 1)(lambda: hello(up))
    pl.when(z > 0)(lambda: hello(down))
    count = count + pick(z < n - 1, 1, 0) + pick(z > 0, 1, 0)
    for a in range(2):
        to_row, _, stays = targets[a]
        pl.when(jnp.logical_not(stays))(lambda to_row=to_row: hello((to_row, to_col)))
        count = count + pick(stays, 0, 1)
        from_row, stays = origins[a]
        pl.when(jnp.logical_not(stays))(lambda from_row=from_row: hello((from_row, from_col)))
        count = count + pick(stays, 0, 1)
    pl.semaphore_wait(barrier, count)

    def keep_half(s, cc):
        rows = pl.ds(pl.multiple_of(cc * h, h), h)
        V[s, rows, :] = X[s, rows, pl.ds(pl.multiple_of(p * half, half), half)]

    def roots(s, zs, cond):
        for q in range(2):
            here = is_root if cond is None else jnp.logical_and(is_root, cond)
            pl.when(here)(lambda q=q: keep_half(s, 2 * zs + q))
            go(here, lambda q=q: v_copy(s, 2 * zs + q, q, False))

    def start_own(s):
        X[s, pl.ds(pl.multiple_of(c * h, h), h), :] = rot[s]
        go(z < n - 1, lambda: x_copy(s, c, 0))
        go(z > 0, lambda: x_copy(s, c, 1))
        go(None, lambda: x_copy(s, c, 2))

    def finish_own(s):
        x_copy(s, 2 * z + 1 - p, 2).wait_recv()
        roots(s, z, None)

    def sides(d):
        return ((0, z - d, z >= d), (1, z + d, z + d < n))

    def service(s, d):
        for way, zs, exists in sides(d):
            cc = 2 * zs + p
            pl.when(exists)(lambda cc=cc, way=way: x_copy(s, cc, way).wait_recv())
            if d < n - 1:
                onward = z < n - 1 if way == 0 else z > 0
                go(jnp.logical_and(exists, onward), lambda cc=cc, way=way: x_copy(s, cc, way))
            go(exists, lambda cc=cc: x_copy(s, cc, 2))
        for way, zs, exists in sides(d):
            cc = 2 * zs + 1 - p
            pl.when(exists)(lambda cc=cc: x_copy(s, cc, 2).wait_recv())
            roots(s, zs, exists)

    def relay(s, d):
        group = ((0, z, None),) if d == 0 else sides(d)
        for _, zs, exists in group:
            for q in range(2):
                cc = 2 * zs + q
                here = jnp.logical_not(is_root)
                if exists is not None:
                    here = jnp.logical_and(here, exists)
                pl.when(here)(lambda cc=cc, q=q: v_copy(s, cc, q, False).wait_recv())
                further = (succ if q == 0 else pred) != z
                go(jnp.logical_and(here, further), lambda cc=cc, q=q: v_copy(s, cc, q, False))

    def split_x(s):
        @pl.loop(0, size // TILE)
        def _(i):
            rows = pl.ds(pl.multiple_of(i * TILE, TILE), TILE)
            hi, lo = split(X[s, rows, :].T)
            Xh[:, rows] = hi
            Xl[:, rows] = lo

    def split_b(load):
        @pl.loop(0, size // TILE)
        def _(i):
            rows = pl.ds(pl.multiple_of(i * TILE, TILE), TILE)
            hi, lo = split(load(rows))
            Bh[rows, :] = hi
            Bl[rows, :] = lo

    def split_v(s):
        columns = pl.ds(pl.multiple_of(p * half, half), half)
        pl.when(is_root)(lambda: split_b(lambda rows: X[s, rows, columns]))
        pl.when(jnp.logical_not(is_root))(lambda: split_b(lambda rows: V[s, rows, :]))

    def t_copy(s, a):
        part = T.at[s, p, pl.ds(a * half, half), :]
        return remote(part, part, tsend.at[s, a], trecv.at[s, a], partner)

    def turn(s):
        for a in range(2):
            @pl.loop(0, half // TILE)
            def _(i):
                rows = pl.ds(pl.multiple_of(a * half + i * TILE, TILE), TILE)
                hi = Xh[rows, :]
                T[s, p, rows, :] = dot(hi, Bh[...]) + dot(hi, Bl[...]) + dot(Xl[rows, :], Bh[...])
            go(None, lambda a=a: t_copy(s, a))

    def m_copy(s, a):
        to_row, slot, _ = targets[a]
        landing = C if s < steps - 1 else out
        dst = landing.at[pl.ds(pl.multiple_of(slot * half, half), half), :] if s == steps - 1 \
            else landing.at[s, pl.ds(pl.multiple_of(slot * half, half), half), :]
        src = res.at[s, pl.ds(a * half, half), :]
        return src, dst, slot, to_row

    def m_remote(s, a):
        src, dst, slot, to_row = m_copy(s, a)
        return remote(src, dst, msend.at[s, a], mrecv.at[s, slot], (to_row, to_col))

    def m_local(s, a):
        src, dst, slot, _ = m_copy(s, a)
        return pltpu.make_async_copy(src, dst, mrecv.at[s, slot])

    def mix(s):
        for a in range(2):
            t_copy(s, a).wait_recv()

            @pl.loop(0, half // TILE)
            def _(i):
                rows = pl.ds(pl.multiple_of(a * half + i * TILE, TILE), TILE)
                total = jnp.zeros((TILE, half), jnp.float32)
                for q in range(2):
                    hi, lo = split(T[s, q, rows, :])
                    bh = Bh[q * half:(q + 1) * half, :]
                    bl = Bl[q * half:(q + 1) * half, :]
                    total = total + (dot(hi, bh) + dot(hi, bl) + dot(lo, bh))
                res[s, rows, :] = total
            stays = targets[a][2]
            pl.when(stays)(lambda a=a: m_local(s, a).start())
            go(jnp.logical_not(stays), lambda a=a: m_remote(s, a))

    def arrive(s):
        for a in range(2):
            src = res.at[s, pl.ds(0, half), :]
            dst = (C.at[s] if s < steps - 1 else out).at[pl.ds(a * half, half), :]
            pltpu.make_async_copy(src, dst, mrecv.at[s, a]).wait()

    start_own(0)
    finish_own(0)
    for d in range(1, n):
        service(0, d)
        if d == n - 2 or n == 2:
            start_own(1)
        if d >= 2:
            relay(0, d - 2)
    split_x(0)
    split_b(lambda rows: gram[rows, :])
    turn(0)
    for d in range(max(n - 2, 0), n - 1):
        relay(0, d)
    finish_own(1)
    service(1, 1)
    relay(0, n - 1)
    split_v(0)
    mix(0)
    for d in range(2, n):
        service(1, d)
        relay(1, d - 2)
    split_x(1)
    for d in range(max(n - 2, 0), n):
        relay(1, d)
    arrive(0)
    split_b(lambda rows: C[0, rows, :])
    turn(1)
    split_v(1)
    mix(1)
    arrive(1)
    for cond, end in pending:
        if cond is None:
            end()
        else:
            pl.when(cond)(end)


def shards(gram, rotations):
    n = lax.axis_size("row")
    n_col = lax.axis_size("col")
    steps, _, h, size = rotations.shape
    half = size // 2
    f32, bf16 = jnp.float32, jnp.bfloat16
    dma = pltpu.SemaphoreType.DMA
    vmem = pl.BlockSpec(memory_space=pltpu.VMEM)
    flops = steps * 2 * 2 * size * size * half * 3
    return pl.pallas_call(
        functools.partial(kernel, n),
        out_shape=jax.ShapeDtypeStruct(gram.shape, f32),
        in_specs=[vmem, vmem],
        out_specs=vmem,
        scratch_shapes=[
            pltpu.VMEM((steps, size, size), f32),
            pltpu.VMEM((steps, size, half), f32),
            pltpu.VMEM((steps, 2, size, half), f32),
            pltpu.VMEM((steps - 1, size, half), f32),
            pltpu.VMEM((steps, size, half), f32),
            pltpu.VMEM((size, size), bf16),
            pltpu.VMEM((size, size), bf16),
            pltpu.VMEM((size, half), bf16),
            pltpu.VMEM((size, half), bf16),
            dma((steps, n_col, 3)),
            dma((steps, n_col)),
            dma((steps, n_col)),
            dma((steps, n_col)),
            dma((steps, 2)),
            dma((steps, 2)),
            dma((steps, 2)),
            dma((steps, 2)),
        ],
        compiler_params=pltpu.CompilerParams(
            collective_id=0, has_side_effects=True, vmem_limit_bytes=56 * 1024 * 1024
        ),
        cost_estimate=pl.CostEstimate(flops=flops, bytes_accessed=8 * 1024 * 1024, transcendentals=0),
    )(gram, rotations.reshape(steps, h, size))


def solution(mesh):
    placed = (P("row", "col"), P(None, "row", "col", None))
    return jax.shard_map(
        shards, mesh=mesh, in_specs=placed, out_specs=P("row", "col"), check_vma=False
    )
```

```python
import functools

import jax
import jax.numpy as jnp
from jax import lax
from jax.experimental import pallas as pl
from jax.experimental.pallas import tpu as pltpu
from jax.sharding import PartitionSpec as P

MESH = pl.DeviceIdType.MESH
TILE = 256


def pick(cond, yes, no):
    return jnp.where(cond, jnp.int32(yes), jnp.int32(no))


def goes_to(n, pair, odd):
    even_pair = pick(pair == 0, 0, pick(pair == n - 1, n - 1, pair + 1))
    even_half = pick(pair == n - 1, 1, 0)
    odd_pair = pick(pair == 0, 1, pair - 1)
    odd_half = pick(pair == 0, 0, 1)
    return pick(odd == 0, even_pair, odd_pair), pick(odd == 0, even_half, odd_half)


def comes_from(n, pair, odd):
    even_pair = pick(pair == 0, 0, pair - 1)
    even_half = pick(pair == 1, 1, 0)
    odd_pair = pick(pair == n - 1, n - 1, pair + 1)
    odd_half = pick(pair == n - 1, 0, 1)
    return pick(odd == 0, even_pair, odd_pair), pick(odd == 0, even_half, odd_half)


def ring_next(n, r, direction):
    order = [i ^ (i >> 1) for i in range(n)]
    result = jnp.int32(0)
    for i in range(n):
        result = pick(r == order[i], order[(i + direction) % n], result)
    return result


def split(x):
    hi = x.astype(jnp.bfloat16)
    lo = (x - hi.astype(jnp.float32)).astype(jnp.bfloat16)
    return hi, lo


def dot(a, b):
    return jnp.dot(a, b, preferred_element_type=jnp.float32)


def kernel(
    n, gram, rot, out, X, V, T, C, res, Xh, Xl, Bh, Bl,
    xsend, xrecv, vsend, vrecv, tsend, trecv, msend, mrecv,
):
    r = lax.axis_index("row")
    c = lax.axis_index("col")
    z = c // 2
    p = c % 2
    steps, h, size = rot.shape
    half = size // 2
    succ = ring_next(n, r, 1)
    pred = ring_next(n, r, -1)
    partner = (r, c + 1 - 2 * p)
    up = (r, c + 2)
    down = (r, c - 2)
    is_root = r == z
    pending = []

    def remote(src, dst, send, recv, device):
        return pltpu.make_async_remote_copy(
            src_ref=src, dst_ref=dst, send_sem=send, recv_sem=recv,
            device_id=device, device_id_type=MESH,
        )

    def x_rows(s, cc):
        return X.at[s, pl.ds(pl.multiple_of(cc * h, h), h), :]

    def x_copy(s, cc, way):
        device = (up, down, partner)[way]
        rows = x_rows(s, cc)
        return remote(rows, rows, xsend.at[s, cc, way], xrecv.at[s, cc], device)

    def v_copy(s, cc, q, root):
        rows = pl.ds(pl.multiple_of(cc * h, h), h)
        dst = V.at[s, rows, :]
        src = X.at[s, rows, pl.ds(pl.multiple_of(p * half, half), half)] if root else dst
        device = ((succ if q == 0 else pred), c)
        return remote(src, dst, vsend.at[s, cc], vrecv.at[s, cc], device)

    def go(cond, make):
        def begin():
            make().start()
        def end():
            make().wait_send()
        if cond is None:
            begin()
        else:
            pl.when(cond)(begin)
        pending.append((cond, end))

    targets = []
    to_pair, to_odd = goes_to(n, z, p)
    to_col = 2 * to_pair + to_odd
    for a in range(2):
        to_row, slot = goes_to(n, r, jnp.int32(a))
        stays = jnp.logical_and(to_row == r, to_col == c)
        targets.append((to_row, slot, stays))
    origins = []
    from_pair, from_odd = comes_from(n, z, p)
    from_col = 2 * from_pair + from_odd
    for a in range(2):
        from_row, _ = comes_from(n, r, jnp.int32(a))
        stays = jnp.logical_and(from_row == r, from_col == c)
        origins.append((from_row, stays))

    barrier = pltpu.get_barrier_semaphore()

    def hello(device):
        pl.semaphore_signal(barrier, inc=1, device_id=device, device_id_type=MESH)

    count = jnp.int32(3)
    hello(partner)
    hello((succ, c))
    hello((pred, c))
    pl.when(z < n - 1)(lambda: hello(up))
    pl.when(z > 0)(lambda: hello(down))
    count = count + pick(z < n - 1, 1, 0) + pick(z > 0, 1, 0)
    for a in range(2):
        to_row, _, stays = targets[a]
        pl.when(jnp.logical_not(stays))(lambda to_row=to_row: hello((to_row, to_col)))
        count = count + pick(stays, 0, 1)
        from_row, stays = origins[a]
        pl.when(jnp.logical_not(stays))(lambda from_row=from_row: hello((from_row, from_col)))
        count = count + pick(stays, 0, 1)
    pl.semaphore_wait(barrier, count)

    def roots(s, zs, cond):
        for q in range(2):
            here = is_root if cond is None else jnp.logical_and(is_root, cond)
            go(here, lambda q=q: v_copy(s, 2 * zs + q, q, True))

    def start_own(s):
        X[s, pl.ds(pl.multiple_of(c * h, h), h), :] = rot[s]
        go(z < n - 1, lambda: x_copy(s, c, 0))
        go(z > 0, lambda: x_copy(s, c, 1))
        go(None, lambda: x_copy(s, c, 2))

    def finish_own(s):
        x_copy(s, 2 * z + 1 - p, 2).wait_recv()
        roots(s, z, None)

    def sides(d):
        return ((0, z - d, z >= d), (1, z + d, z + d < n))

    def service(s, d):
        for way, zs, exists in sides(d):
            cc = 2 * zs + p
            pl.when(exists)(lambda cc=cc, way=way: x_copy(s, cc, way).wait_recv())
            if d < n - 1:
                onward = z < n - 1 if way == 0 else z > 0
                go(jnp.logical_and(exists, onward), lambda cc=cc, way=way: x_copy(s, cc, way))
            go(exists, lambda cc=cc: x_copy(s, cc, 2))
        for way, zs, exists in sides(d):
            cc = 2 * zs + 1 - p
            pl.when(exists)(lambda cc=cc: x_copy(s, cc, 2).wait_recv())
            roots(s, zs, exists)

    def v_shards(d):
        group = ((0, z, None),) if d == 0 else sides(d)
        for _, zs, exists in group:
            for q in range(2):
                here = jnp.logical_not(is_root)
                if exists is not None:
                    here = jnp.logical_and(here, exists)
                yield 2 * zs + q, q, here, (succ if q == 0 else pred) != z

    def relay(s, d):
        for cc, q, here, further in v_shards(d):
            onward = jnp.logical_and(here, further)
            pl.when(onward)(lambda cc=cc, q=q: v_copy(s, cc, q, False).wait_recv())
            go(onward, lambda cc=cc, q=q: v_copy(s, cc, q, False))

    def finish_v(s):
        for d in range(n):
            for cc, q, here, further in v_shards(d):
                ends = jnp.logical_and(here, jnp.logical_not(further))
                pl.when(ends)(lambda cc=cc, q=q: v_copy(s, cc, q, False).wait_recv())

    def split_x(s):
        @pl.loop(0, size // TILE)
        def _(i):
            rows = pl.ds(pl.multiple_of(i * TILE, TILE), TILE)
            hi, lo = split(X[s, rows, :].T)
            Xh[:, rows] = hi
            Xl[:, rows] = lo

    def split_b(load):
        @pl.loop(0, size // TILE)
        def _(i):
            rows = pl.ds(pl.multiple_of(i * TILE, TILE), TILE)
            hi, lo = split(load(rows))
            Bh[rows, :] = hi
            Bl[rows, :] = lo

    def split_v(s):
        columns = pl.ds(pl.multiple_of(p * half, half), half)
        pl.when(is_root)(lambda: split_b(lambda rows: X[s, rows, columns]))
        pl.when(jnp.logical_not(is_root))(lambda: split_b(lambda rows: V[s, rows, :]))

    def t_copy(s, a):
        part = T.at[s, p, pl.ds(a * half, half), :]
        return remote(part, part, tsend.at[s, a], trecv.at[s, a], partner)

    def turn(s):
        for a in range(2):
            @pl.loop(0, half // TILE)
            def _(i):
                rows = pl.ds(pl.multiple_of(a * half + i * TILE, TILE), TILE)
                hi = Xh[rows, :]
                T[s, p, rows, :] = dot(hi, Bh[...]) + dot(hi, Bl[...]) + dot(Xl[rows, :], Bh[...])
            go(None, lambda a=a: t_copy(s, a))

    def m_copy(s, a):
        to_row, slot, _ = targets[a]
        landing = C if s < steps - 1 else out
        dst = landing.at[pl.ds(pl.multiple_of(slot * half, half), half), :] if s == steps - 1 \
            else landing.at[s, pl.ds(pl.multiple_of(slot * half, half), half), :]
        src = res.at[s, pl.ds(a * half, half), :]
        return src, dst, slot, to_row

    def m_remote(s, a):
        src, dst, slot, to_row = m_copy(s, a)
        return remote(src, dst, msend.at[s, a], mrecv.at[s, slot], (to_row, to_col))

    def m_local(s, a):
        src, dst, slot, _ = m_copy(s, a)
        return pltpu.make_async_copy(src, dst, mrecv.at[s, slot])

    def mix(s):
        for a in range(2):
            t_copy(s, a).wait_recv()

            @pl.loop(0, half // TILE)
            def _(i):
                rows = pl.ds(pl.multiple_of(a * half + i * TILE, TILE), TILE)
                total = jnp.zeros((TILE, half), jnp.float32)
                for q in range(2):
                    hi, lo = split(T[s, q, rows, :])
                    bh = Bh[q * half:(q + 1) * half, :]
                    bl = Bl[q * half:(q + 1) * half, :]
                    total = total + (dot(hi, bh) + dot(hi, bl) + dot(lo, bh))
                res[s, rows, :] = total
            stays = targets[a][2]
            pl.when(stays)(lambda a=a: m_local(s, a).start())
            go(jnp.logical_not(stays), lambda a=a: m_remote(s, a))

    def arrive(s):
        for a in range(2):
            src = res.at[s, pl.ds(0, half), :]
            dst = (C.at[s] if s < steps - 1 else out).at[pl.ds(a * half, half), :]
            pltpu.make_async_copy(src, dst, mrecv.at[s, a]).wait()

    start_own(0)
    finish_own(0)
    for d in range(1, n):
        service(0, d)
        if d == n - 2 or n == 2:
            start_own(1)
        relay(0, d - 1)
    split_x(0)
    split_b(lambda rows: gram[rows, :])
    relay(0, n - 1)
    turn(0)
    finish_own(1)
    service(1, 1)
    relay(1, 0)
    finish_v(0)
    split_v(0)
    mix(0)
    for d in range(2, n):
        service(1, d)
        relay(1, d - 1)
    split_x(1)
    relay(1, n - 1)
    arrive(0)
    split_b(lambda rows: C[0, rows, :])
    turn(1)
    finish_v(1)
    split_v(1)
    mix(1)
    arrive(1)
    for cond, end in pending:
        if cond is None:
            end()
        else:
            pl.when(cond)(end)


def shards(gram, rotations):
    n = lax.axis_size("row")
    n_col = lax.axis_size("col")
    steps, _, h, size = rotations.shape
    half = size // 2
    f32, bf16 = jnp.float32, jnp.bfloat16
    dma = pltpu.SemaphoreType.DMA
    vmem = pl.BlockSpec(memory_space=pltpu.VMEM)
    flops = steps * 2 * 2 * size * size * half * 3
    return pl.pallas_call(
        functools.partial(kernel, n),
        out_shape=jax.ShapeDtypeStruct(gram.shape, f32),
        in_specs=[vmem, vmem],
        out_specs=vmem,
        scratch_shapes=[
            pltpu.VMEM((steps, size, size), f32),
            pltpu.VMEM((steps, size, half), f32),
            pltpu.VMEM((steps, 2, size, half), f32),
            pltpu.VMEM((steps - 1, size, half), f32),
            pltpu.VMEM((steps, size, half), f32),
            pltpu.VMEM((size, size), bf16),
            pltpu.VMEM((size, size), bf16),
            pltpu.VMEM((size, half), bf16),
            pltpu.VMEM((size, half), bf16),
            dma((steps, n_col, 3)),
            dma((steps, n_col)),
            dma((steps, n_col)),
            dma((steps, n_col)),
            dma((steps, 2)),
            dma((steps, 2)),
            dma((steps, 2)),
            dma((steps, 2)),
        ],
        compiler_params=pltpu.CompilerParams(
            collective_id=0, has_side_effects=True, vmem_limit_bytes=56 * 1024 * 1024
        ),
        cost_estimate=pl.CostEstimate(flops=flops, bytes_accessed=8 * 1024 * 1024, transcendentals=0),
    )(gram, rotations.reshape(steps, h, size))


def solution(mesh):
    placed = (P("row", "col"), P(None, "row", "col", None))
    return jax.shard_map(
        shards, mesh=mesh, in_specs=placed, out_specs=P("row", "col"), check_vma=False
    )
```

```python
import functools

import jax
import jax.numpy as jnp
from jax import lax
from jax.experimental import pallas as pl
from jax.experimental.pallas import tpu as pltpu
from jax.sharding import PartitionSpec as P

MESH = pl.DeviceIdType.MESH
TILE = 256


def pick(cond, yes, no):
    return jnp.where(cond, jnp.int32(yes), jnp.int32(no))


def goes_to(n, pair, odd):
    even_pair = pick(pair == 0, 0, pick(pair == n - 1, n - 1, pair + 1))
    even_half = pick(pair == n - 1, 1, 0)
    odd_pair = pick(pair == 0, 1, pair - 1)
    odd_half = pick(pair == 0, 0, 1)
    return pick(odd == 0, even_pair, odd_pair), pick(odd == 0, even_half, odd_half)


def comes_from(n, pair, odd):
    even_pair = pick(pair == 0, 0, pair - 1)
    even_half = pick(pair == 1, 1, 0)
    odd_pair = pick(pair == n - 1, n - 1, pair + 1)
    odd_half = pick(pair == n - 1, 0, 1)
    return pick(odd == 0, even_pair, odd_pair), pick(odd == 0, even_half, odd_half)


def ring_next(n, r, direction):
    order = [i ^ (i >> 1) for i in range(n)]
    result = jnp.int32(0)
    for i in range(n):
        result = pick(r == order[i], order[(i + direction) % n], result)
    return result


def split(x):
    hi = x.astype(jnp.bfloat16)
    lo = (x - hi.astype(jnp.float32)).astype(jnp.bfloat16)
    return hi, lo


def dot(a, b):
    return jnp.dot(a, b, preferred_element_type=jnp.float32)


def kernel(
    n, gram, rot, out, X, V, T, C, res, Xh, Xl, Bh, Bl,
    xsend, xrecv, vsend, vrecv, tsend, trecv, msend, mrecv,
):
    r = lax.axis_index("row")
    c = lax.axis_index("col")
    z = c // 2
    p = c % 2
    steps, h, size = rot.shape
    half = size // 2
    succ = ring_next(n, r, 1)
    pred = ring_next(n, r, -1)
    partner = (r, c + 1 - 2 * p)
    up = (r, c + 2)
    down = (r, c - 2)
    is_root = r == z
    pending = []

    def remote(src, dst, send, recv, device):
        return pltpu.make_async_remote_copy(
            src_ref=src, dst_ref=dst, send_sem=send, recv_sem=recv,
            device_id=device, device_id_type=MESH,
        )

    def x_rows(s, cc):
        return X.at[s, pl.ds(pl.multiple_of(cc * h, h), h), :]

    def x_copy(s, cc, way):
        device = (up, down, partner)[way]
        rows = x_rows(s, cc)
        return remote(rows, rows, xsend.at[s, cc, way], xrecv.at[s, cc], device)

    def v_copy(s, cc, q, root):
        rows = pl.ds(pl.multiple_of(cc * h, h), h)
        dst = V.at[s, rows, :]
        src = X.at[s, rows, pl.ds(pl.multiple_of(p * half, half), half)] if root else dst
        device = ((succ if q == 0 else pred), c)
        return remote(src, dst, vsend.at[s, cc], vrecv.at[s, cc], device)

    def go(cond, make):
        def begin():
            make().start()
        def end():
            make().wait_send()
        if cond is None:
            begin()
        else:
            pl.when(cond)(begin)
        pending.append((cond, end))

    targets = []
    to_pair, to_odd = goes_to(n, z, p)
    to_col = 2 * to_pair + to_odd
    for a in range(2):
        to_row, slot = goes_to(n, r, jnp.int32(a))
        stays = jnp.logical_and(to_row == r, to_col == c)
        targets.append((to_row, slot, stays))
    origins = []
    from_pair, from_odd = comes_from(n, z, p)
    from_col = 2 * from_pair + from_odd
    for a in range(2):
        from_row, _ = comes_from(n, r, jnp.int32(a))
        stays = jnp.logical_and(from_row == r, from_col == c)
        origins.append((from_row, stays))

    barrier = pltpu.get_barrier_semaphore()

    def hello(device):
        pl.semaphore_signal(barrier, inc=1, device_id=device, device_id_type=MESH)

    count = jnp.int32(3)
    hello(partner)
    hello((succ, c))
    hello((pred, c))
    pl.when(z < n - 1)(lambda: hello(up))
    pl.when(z > 0)(lambda: hello(down))
    count = count + pick(z < n - 1, 1, 0) + pick(z > 0, 1, 0)
    for a in range(2):
        to_row, _, stays = targets[a]
        pl.when(jnp.logical_not(stays))(lambda to_row=to_row: hello((to_row, to_col)))
        count = count + pick(stays, 0, 1)
        from_row, stays = origins[a]
        pl.when(jnp.logical_not(stays))(lambda from_row=from_row: hello((from_row, from_col)))
        count = count + pick(stays, 0, 1)
    pl.semaphore_wait(barrier, count)

    def roots(s, zs, cond):
        for q in range(2):
            here = is_root if cond is None else jnp.logical_and(is_root, cond)
            go(here, lambda q=q: v_copy(s, 2 * zs + q, q, True))

    def start_own(s):
        X[s, pl.ds(pl.multiple_of(c * h, h), h), :] = rot[s]
        go(z < n - 1, lambda: x_copy(s, c, 0))
        go(z > 0, lambda: x_copy(s, c, 1))
        go(None, lambda: x_copy(s, c, 2))

    def finish_own(s):
        x_copy(s, 2 * z + 1 - p, 2).wait_recv()
        roots(s, z, None)

    def sides(d):
        return ((0, z - d, z >= d), (1, z + d, z + d < n))

    def service(s, d):
        for way, zs, exists in sides(d):
            cc = 2 * zs + p
            pl.when(exists)(lambda cc=cc, way=way: x_copy(s, cc, way).wait_recv())
            if d < n - 1:
                onward = z < n - 1 if way == 0 else z > 0
                go(jnp.logical_and(exists, onward), lambda cc=cc, way=way: x_copy(s, cc, way))
            go(exists, lambda cc=cc: x_copy(s, cc, 2))
        for way, zs, exists in sides(d):
            cc = 2 * zs + 1 - p
            pl.when(exists)(lambda cc=cc: x_copy(s, cc, 2).wait_recv())
            roots(s, zs, exists)

    def v_shards(d):
        group = ((0, z, None),) if d == 0 else sides(d)
        for _, zs, exists in group:
            for q in range(2):
                here = jnp.logical_not(is_root)
                if exists is not None:
                    here = jnp.logical_and(here, exists)
                yield 2 * zs + q, q, here, (succ if q == 0 else pred) != z

    def relay(s, d):
        for cc, q, here, further in v_shards(d):
            onward = jnp.logical_and(here, further)
            pl.when(onward)(lambda cc=cc, q=q: v_copy(s, cc, q, False).wait_recv())
            go(onward, lambda cc=cc, q=q: v_copy(s, cc, q, False))

    def finish_v(s):
        for d in range(n):
            for cc, q, here, further in v_shards(d):
                ends = jnp.logical_and(here, jnp.logical_not(further))
                pl.when(ends)(lambda cc=cc, q=q: v_copy(s, cc, q, False).wait_recv())

    def split_x(s):
        @pl.loop(0, size // TILE)
        def _(i):
            rows = pl.ds(pl.multiple_of(i * TILE, TILE), TILE)
            hi, lo = split(X[s, rows, :].T)
            Xh[:, rows] = hi
            Xl[:, rows] = lo

    def split_b(load):
        @pl.loop(0, size // TILE)
        def _(i):
            rows = pl.ds(pl.multiple_of(i * TILE, TILE), TILE)
            hi, lo = split(load(rows))
            Bh[rows, :] = hi
            Bl[rows, :] = lo

    def split_v(s):
        columns = pl.ds(pl.multiple_of(p * half, half), half)
        pl.when(is_root)(lambda: split_b(lambda rows: X[s, rows, columns]))
        pl.when(jnp.logical_not(is_root))(lambda: split_b(lambda rows: V[s, rows, :]))

    def t_copy(s, a):
        part = T.at[s, p, pl.ds(a * half, half), :]
        return remote(part, part, tsend.at[s, a], trecv.at[s, a], partner)

    def turn(s):
        for a in range(2):
            @pl.loop(0, half // TILE)
            def _(i):
                rows = pl.ds(pl.multiple_of(a * half + i * TILE, TILE), TILE)
                hi = Xh[rows, :]
                T[s, p, rows, :] = dot(hi, Bh[...]) + dot(hi, Bl[...]) + dot(Xl[rows, :], Bh[...])
            go(None, lambda a=a: t_copy(s, a))

    def m_copy(s, a, i):
        to_row, slot, _ = targets[a]
        landing = C.at[s] if s < steps - 1 else out
        dst = landing.at[pl.ds(pl.multiple_of(slot * half + i * TILE, TILE), TILE), :]
        src = res.at[s, pl.ds(a * half + i * TILE, TILE), :]
        return src, dst, slot, to_row

    def m_remote(s, a, i):
        src, dst, slot, to_row = m_copy(s, a, i)
        return remote(src, dst, msend.at[s, a, i], mrecv.at[s, slot, i], (to_row, to_col))

    def m_local(s, a, i):
        src, dst, slot, _ = m_copy(s, a, i)
        return pltpu.make_async_copy(src, dst, mrecv.at[s, slot, i])

    def mix(s):
        for a in range(2):
            t_copy(s, a).wait_recv()
            stays = targets[a][2]
            for i in range(half // TILE):
                rows = pl.ds(a * half + i * TILE, TILE)
                total = jnp.zeros((TILE, half), jnp.float32)
                for q in range(2):
                    hi, lo = split(T[s, q, rows, :])
                    bh = Bh[q * half:(q + 1) * half, :]
                    bl = Bl[q * half:(q + 1) * half, :]
                    total = total + (dot(hi, bh) + dot(hi, bl) + dot(lo, bh))
                res[s, rows, :] = total
                pl.when(stays)(lambda a=a, i=i: m_local(s, a, i).start())
                go(jnp.logical_not(stays), lambda a=a, i=i: m_remote(s, a, i))

    def arrive(s):
        for a in range(2):
            for i in range(half // TILE):
                src = res.at[s, pl.ds(0, TILE), :]
                dst = (C.at[s] if s < steps - 1 else out).at[pl.ds(a * half + i * TILE, TILE), :]
                pltpu.make_async_copy(src, dst, mrecv.at[s, a, i]).wait()

    start_own(0)
    finish_own(0)
    for d in range(1, n):
        service(0, d)
        if d == n - 2 or n == 2:
            start_own(1)
        relay(0, d - 1)
    split_x(0)
    split_b(lambda rows: gram[rows, :])
    relay(0, n - 1)
    turn(0)
    finish_own(1)
    service(1, 1)
    relay(1, 0)
    finish_v(0)
    split_v(0)
    mix(0)
    for d in range(2, n):
        service(1, d)
        relay(1, d - 1)
    split_x(1)
    relay(1, n - 1)
    arrive(0)
    split_b(lambda rows: C[0, rows, :])
    turn(1)
    finish_v(1)
    split_v(1)
    mix(1)
    arrive(1)
    for cond, end in pending:
        if cond is None:
            end()
        else:
            pl.when(cond)(end)


def shards(gram, rotations):
    n = lax.axis_size("row")
    n_col = lax.axis_size("col")
    steps, _, h, size = rotations.shape
    half = size // 2
    f32, bf16 = jnp.float32, jnp.bfloat16
    dma = pltpu.SemaphoreType.DMA
    vmem = pl.BlockSpec(memory_space=pltpu.VMEM)
    flops = steps * 2 * 2 * size * size * half * 3
    return pl.pallas_call(
        functools.partial(kernel, n),
        out_shape=jax.ShapeDtypeStruct(gram.shape, f32),
        in_specs=[vmem, vmem],
        out_specs=vmem,
        scratch_shapes=[
            pltpu.VMEM((steps, size, size), f32),
            pltpu.VMEM((steps, size, half), f32),
            pltpu.VMEM((steps, 2, size, half), f32),
            pltpu.VMEM((steps - 1, size, half), f32),
            pltpu.VMEM((steps, size, half), f32),
            pltpu.VMEM((size, size), bf16),
            pltpu.VMEM((size, size), bf16),
            pltpu.VMEM((size, half), bf16),
            pltpu.VMEM((size, half), bf16),
            dma((steps, n_col, 3)),
            dma((steps, n_col)),
            dma((steps, n_col)),
            dma((steps, n_col)),
            dma((steps, 2)),
            dma((steps, 2)),
            dma((steps, 2, half // TILE)),
            dma((steps, 2, half // TILE)),
        ],
        compiler_params=pltpu.CompilerParams(
            collective_id=0, has_side_effects=True, vmem_limit_bytes=56 * 1024 * 1024
        ),
        cost_estimate=pl.CostEstimate(flops=flops, bytes_accessed=8 * 1024 * 1024, transcendentals=0),
    )(gram, rotations.reshape(steps, h, size))


def solution(mesh):
    placed = (P("row", "col"), P(None, "row", "col", None))
    return jax.shard_map(
        shards, mesh=mesh, in_specs=placed, out_specs=P("row", "col"), check_vma=False
    )
```

```python
import functools

import jax
import jax.numpy as jnp
from jax import lax
from jax.experimental import pallas as pl
from jax.experimental.pallas import tpu as pltpu
from jax.sharding import PartitionSpec as P

MESH = pl.DeviceIdType.MESH
TILE = 256


def pick(cond, yes, no):
    return jnp.where(cond, jnp.int32(yes), jnp.int32(no))


def goes_to(n, pair, odd):
    even_pair = pick(pair == 0, 0, pick(pair == n - 1, n - 1, pair + 1))
    even_half = pick(pair == n - 1, 1, 0)
    odd_pair = pick(pair == 0, 1, pair - 1)
    odd_half = pick(pair == 0, 0, 1)
    return pick(odd == 0, even_pair, odd_pair), pick(odd == 0, even_half, odd_half)


def comes_from(n, pair, odd):
    even_pair = pick(pair == 0, 0, pair - 1)
    even_half = pick(pair == 1, 1, 0)
    odd_pair = pick(pair == n - 1, n - 1, pair + 1)
    odd_half = pick(pair == n - 1, 0, 1)
    return pick(odd == 0, even_pair, odd_pair), pick(odd == 0, even_half, odd_half)


def ring_next(n, r, direction):
    order = [i ^ (i >> 1) for i in range(n)]
    result = jnp.int32(0)
    for i in range(n):
        result = pick(r == order[i], order[(i + direction) % n], result)
    return result


def split(x):
    hi = x.astype(jnp.bfloat16)
    lo = (x - hi.astype(jnp.float32)).astype(jnp.bfloat16)
    return hi, lo


def dot(a, b):
    return jnp.dot(a, b, preferred_element_type=jnp.float32)


def kernel(
    n, gram, rot, out, X, V, T, C, res, Xh, Xl, Bh, Bl,
    xsend, xrecv, vsend, vrecv, tsend, trecv, msend, mrecv,
):
    r = lax.axis_index("row")
    c = lax.axis_index("col")
    z = c // 2
    p = c % 2
    steps, h, size = rot.shape
    half = size // 2
    succ = ring_next(n, r, 1)
    pred = ring_next(n, r, -1)
    partner = (r, c + 1 - 2 * p)
    up = (r, c + 2)
    down = (r, c - 2)
    is_root = r == z
    pending = []

    def remote(src, dst, send, recv, device):
        return pltpu.make_async_remote_copy(
            src_ref=src, dst_ref=dst, send_sem=send, recv_sem=recv,
            device_id=device, device_id_type=MESH,
        )

    def x_rows(s, cc):
        return X.at[s, pl.ds(pl.multiple_of(cc * h, h), h), :]

    def x_copy(s, cc, way):
        device = (up, down, partner)[way]
        rows = x_rows(s, cc)
        return remote(rows, rows, xsend.at[s, cc, way], xrecv.at[s, cc], device)

    def v_copy(s, cc, q, root):
        rows = pl.ds(pl.multiple_of(cc * h, h), h)
        dst = V.at[s, rows, :]
        src = X.at[s, rows, pl.ds(pl.multiple_of(p * half, half), half)] if root else dst
        device = ((succ if q == 0 else pred), c)
        return remote(src, dst, vsend.at[s, cc], vrecv.at[s, cc], device)

    def go(cond, make):
        def begin():
            make().start()
        def end():
            make().wait_send()
        if cond is None:
            begin()
        else:
            pl.when(cond)(begin)
        pending.append((cond, end))

    targets = []
    to_pair, to_odd = goes_to(n, z, p)
    to_col = 2 * to_pair + to_odd
    for a in range(2):
        to_row, slot = goes_to(n, r, jnp.int32(a))
        stays = jnp.logical_and(to_row == r, to_col == c)
        targets.append((to_row, slot, stays))
    origins = []
    from_pair, from_odd = comes_from(n, z, p)
    from_col = 2 * from_pair + from_odd
    for a in range(2):
        from_row, _ = comes_from(n, r, jnp.int32(a))
        stays = jnp.logical_and(from_row == r, from_col == c)
        origins.append((from_row, stays))

    barrier = pltpu.get_barrier_semaphore()

    def hello(device):
        pl.semaphore_signal(barrier, inc=1, device_id=device, device_id_type=MESH)

    count = jnp.int32(3)
    hello(partner)
    hello((succ, c))
    hello((pred, c))
    pl.when(z < n - 1)(lambda: hello(up))
    pl.when(z > 0)(lambda: hello(down))
    count = count + pick(z < n - 1, 1, 0) + pick(z > 0, 1, 0)
    for a in range(2):
        to_row, _, stays = targets[a]
        pl.when(jnp.logical_not(stays))(lambda to_row=to_row: hello((to_row, to_col)))
        count = count + pick(stays, 0, 1)
        from_row, stays = origins[a]
        pl.when(jnp.logical_not(stays))(lambda from_row=from_row: hello((from_row, from_col)))
        count = count + pick(stays, 0, 1)
    pl.semaphore_wait(barrier, count)

    def roots(s, zs, cond):
        for q in range(2):
            here = is_root if cond is None else jnp.logical_and(is_root, cond)
            go(here, lambda q=q: v_copy(s, 2 * zs + q, q, True))

    def start_own(s):
        X[s, pl.ds(pl.multiple_of(c * h, h), h), :] = rot[s]
        go(z < n - 1, lambda: x_copy(s, c, 0))
        go(z > 0, lambda: x_copy(s, c, 1))
        go(None, lambda: x_copy(s, c, 2))

    def finish_own(s):
        x_copy(s, 2 * z + 1 - p, 2).wait_recv()
        roots(s, z, None)

    def sides(d):
        return ((0, z - d, z >= d), (1, z + d, z + d < n))

    def service(s, d):
        for way, zs, exists in sides(d):
            cc = 2 * zs + p
            pl.when(exists)(lambda cc=cc, way=way: x_copy(s, cc, way).wait_recv())
            if d < n - 1:
                onward = z < n - 1 if way == 0 else z > 0
                go(jnp.logical_and(exists, onward), lambda cc=cc, way=way: x_copy(s, cc, way))
            go(exists, lambda cc=cc: x_copy(s, cc, 2))
        for way, zs, exists in sides(d):
            cc = 2 * zs + 1 - p
            pl.when(exists)(lambda cc=cc: x_copy(s, cc, 2).wait_recv())
            roots(s, zs, exists)

    def v_shards(d):
        group = ((0, z, None),) if d == 0 else sides(d)
        for _, zs, exists in group:
            for q in range(2):
                here = jnp.logical_not(is_root)
                if exists is not None:
                    here = jnp.logical_and(here, exists)
                yield 2 * zs + q, q, here, (succ if q == 0 else pred) != z

    def relay(s, d):
        for cc, q, here, further in v_shards(d):
            onward = jnp.logical_and(here, further)
            pl.when(onward)(lambda cc=cc, q=q: v_copy(s, cc, q, False).wait_recv())
            go(onward, lambda cc=cc, q=q: v_copy(s, cc, q, False))

    def finish_v(s):
        for d in range(n):
            for cc, q, here, further in v_shards(d):
                ends = jnp.logical_and(here, jnp.logical_not(further))
                pl.when(ends)(lambda cc=cc, q=q: v_copy(s, cc, q, False).wait_recv())

    def split_x(s):
        @pl.loop(0, size // TILE)
        def _(i):
            rows = pl.ds(pl.multiple_of(i * TILE, TILE), TILE)
            hi, lo = split(X[s, rows, :].T)
            Xh[:, rows] = hi
            Xl[:, rows] = lo

    def split_b(load):
        @pl.loop(0, size // TILE)
        def _(i):
            rows = pl.ds(pl.multiple_of(i * TILE, TILE), TILE)
            hi, lo = split(load(rows))
            Bh[rows, :] = hi
            Bl[rows, :] = lo

    def split_v(s):
        columns = pl.ds(pl.multiple_of(p * half, half), half)
        pl.when(is_root)(lambda: split_b(lambda rows: X[s, rows, columns]))
        pl.when(jnp.logical_not(is_root))(lambda: split_b(lambda rows: V[s, rows, :]))

    def t_copy(s, a):
        part = T.at[s, p, pl.ds(a * half, half), :]
        return remote(part, part, tsend.at[s, a], trecv.at[s, a], partner)

    def turn(s):
        for a in range(2):
            @pl.loop(0, half // TILE)
            def _(i):
                rows = pl.ds(pl.multiple_of(a * half + i * TILE, TILE), TILE)
                hi = Xh[rows, :]
                T[s, p, rows, :] = dot(hi, Bh[...]) + dot(hi, Bl[...]) + dot(Xl[rows, :], Bh[...])
            go(None, lambda a=a: t_copy(s, a))

    def m_copy(s, a, i):
        to_row, slot, _ = targets[a]
        landing = C.at[s] if s < steps - 1 else out
        dst = landing.at[pl.ds(pl.multiple_of(slot * half + i * TILE, TILE), TILE), :]
        src = res.at[s, pl.ds(a * half + i * TILE, TILE), :]
        return src, dst, slot, to_row

    def m_remote(s, a, i):
        src, dst, slot, to_row = m_copy(s, a, i)
        return remote(src, dst, msend.at[s, a, i], mrecv.at[s, slot, i], (to_row, to_col))

    def m_local(s, a, i):
        src, dst, slot, _ = m_copy(s, a, i)
        return pltpu.make_async_copy(src, dst, mrecv.at[s, slot, i])

    def mix(s):
        for a in range(2):
            t_copy(s, a).wait_recv()
            stays = targets[a][2]
            for i in range(half // TILE):
                rows = pl.ds(a * half + i * TILE, TILE)
                total = jnp.zeros((TILE, half), jnp.float32)
                for q in range(2):
                    hi, lo = split(T[s, q, rows, :])
                    bh = Bh[q * half:(q + 1) * half, :]
                    bl = Bl[q * half:(q + 1) * half, :]
                    total = total + (dot(hi, bh) + dot(hi, bl) + dot(lo, bh))
                res[s, rows, :] = total
                pl.when(stays)(lambda a=a, i=i: m_local(s, a, i).start())
                go(jnp.logical_not(stays), lambda a=a, i=i: m_remote(s, a, i))

    def arrive(s):
        for a in range(2):
            for i in range(half // TILE):
                src = res.at[s, pl.ds(0, TILE), :]
                dst = (C.at[s] if s < steps - 1 else out).at[pl.ds(a * half + i * TILE, TILE), :]
                pltpu.make_async_copy(src, dst, mrecv.at[s, a, i]).wait()

    start_own(0)
    finish_own(0)
    for d in range(1, n):
        service(0, d)
        if d == n - 2 or n == 2:
            start_own(1)
        relay(0, d - 1)
    split_x(0)
    split_b(lambda rows: gram[rows, :])
    relay(0, n - 1)
    turn(0)
    finish_own(1)
    service(1, 1)
    finish_v(0)
    split_v(0)
    mix(0)
    relay(1, 0)
    for d in range(2, n):
        service(1, d)
        relay(1, d - 1)
    split_x(1)
    relay(1, n - 1)
    arrive(0)
    split_b(lambda rows: C[0, rows, :])
    turn(1)
    finish_v(1)
    split_v(1)
    mix(1)
    arrive(1)
    for cond, end in pending:
        if cond is None:
            end()
        else:
            pl.when(cond)(end)


def shards(gram, rotations):
    n = lax.axis_size("row")
    n_col = lax.axis_size("col")
    steps, _, h, size = rotations.shape
    half = size // 2
    f32, bf16 = jnp.float32, jnp.bfloat16
    dma = pltpu.SemaphoreType.DMA
    vmem = pl.BlockSpec(memory_space=pltpu.VMEM)
    flops = steps * 2 * 2 * size * size * half * 3
    return pl.pallas_call(
        functools.partial(kernel, n),
        out_shape=jax.ShapeDtypeStruct(gram.shape, f32),
        in_specs=[vmem, vmem],
        out_specs=vmem,
        scratch_shapes=[
            pltpu.VMEM((steps, size, size), f32),
            pltpu.VMEM((steps, size, half), f32),
            pltpu.VMEM((steps, 2, size, half), f32),
            pltpu.VMEM((steps - 1, size, half), f32),
            pltpu.VMEM((steps, size, half), f32),
            pltpu.VMEM((size, size), bf16),
            pltpu.VMEM((size, size), bf16),
            pltpu.VMEM((size, half), bf16),
            pltpu.VMEM((size, half), bf16),
            dma((steps, n_col, 3)),
            dma((steps, n_col)),
            dma((steps, n_col)),
            dma((steps, n_col)),
            dma((steps, 2)),
            dma((steps, 2)),
            dma((steps, 2, half // TILE)),
            dma((steps, 2, half // TILE)),
        ],
        compiler_params=pltpu.CompilerParams(
            collective_id=0, has_side_effects=True, vmem_limit_bytes=56 * 1024 * 1024
        ),
        cost_estimate=pl.CostEstimate(flops=flops, bytes_accessed=8 * 1024 * 1024, transcendentals=0),
    )(gram, rotations.reshape(steps, h, size))


def solution(mesh):
    placed = (P("row", "col"), P(None, "row", "col", None))
    return jax.shard_map(
        shards, mesh=mesh, in_specs=placed, out_specs=P("row", "col"), check_vma=False
    )
```
